32 devices in a mesh: scen: 8 (over z, y), tile: 4 (over x, core).
Axes of the slice: x: 2, y: 2, z: 4, core: 2. Of those that a mesh axis runs over, the one named last changes fastest.
Arguments:
- factor_inv: bfloat16 [64, 768, 768], P('scen'), may hold values from -0.21875 to 0.21875
- pattern: int32 [64, 6, 6], P('scen'), may hold values 0 or 1
- border: bfloat16 [64, 768, 512], P('scen', None, 'tile'), may hold values from -0.59765625 to 0.59765625
- row_scale: float32 [64, 768], P('scen'), may hold values from 0.25 to 4
- link_ids: int32 [64, 4], P('scen'), may hold values from 0 to 63, as said below
- first_diag: float32 [8192], replicated, may hold values from 10 to 100
Outputs:
- schur: float32 [8192, 8192], P('tile', 'scen')
The draws below stay inside these ranges and needn't reach their ends.
Inputs may be any that keep to these rules, and one draw needn't show every extreme that they name: link_ids[s, j] lies in group j, that is among blocks j * 16 to (j + 1) * 16 - 1. For each aligned block of 8 scenarios and each group, at most 6 of those scenarios link to one run of 8 blocks starting at a multiple of 8, and one such run has exactly 6.
All inputs are finite; a program needn't handle non-finite values. No bound on the sum of `pattern` on one device may be relied on, other than what follows from the above.
Results may differ from the reference program's by a relative error of at most 0.003.
Values may be sent and summed in bfloat16 or wider, within the bound.
A program may use at most 128 MiB of HBM per device.

```python
import math
import jax
import jax.numpy as jnp
from jax import lax

BS = 128
NBLK = 6
SROWS = 768
ORDER = 8192
SC_DEV = 8
SCEN = 64
GROUPS = 4
GROUP_BLK = 16
OWN_BLK = 8
OPG = 2
CAP = 6
N_SCEN = 8


def draw_link_ids(key, part):
    key_heavy, key_offset, key_order, key_sub = jax.random.split(key, 4)
    heavy_owner = jax.random.randint(key_heavy, (N_SCEN, GROUPS), 0, OPG)
    offset_draw = jax.random.randint(key_offset, (N_SCEN, GROUPS), 0, OPG - 1)
    position = jnp.arange(SC_DEV)
    rest_index = jnp.maximum(position - CAP, 0)
    other_owner = (heavy_owner[:, :, None] + 1 + (offset_draw[:, :, None] + rest_index[None, None, :]) % (OPG - 1)) % OPG
    owner_seq = jnp.where(position[None, None, :] < CAP, heavy_owner[:, :, None], other_owner)
    sort_keys = jax.random.randint(key_order, (N_SCEN, GROUPS, SC_DEV), 0, 1048576) * SC_DEV + position[None, None, :]
    order_index = jnp.argsort(sort_keys, axis=-1)
    owner_final = jnp.take_along_axis(owner_seq, order_index, axis=-1)
    sub_block = jax.random.randint(key_sub, (N_SCEN, GROUPS, SC_DEV), 0, OWN_BLK)
    group_index = jnp.arange(GROUPS)[None, :, None]
    link_block = group_index * GROUP_BLK + owner_final * OWN_BLK + sub_block
    return jnp.transpose(link_block, (0, 2, 1)).reshape(SCEN, GROUPS).astype(jnp.int32)


def plant(result, rng, smallest, high):
    place = [jax.random.randint(jax.random.fold_in(rng, axis), (), 0, length) for axis, length in enumerate(result.shape)]
    longest = result.shape.index(max(result.shape))
    beside = place[:longest] + [(place[longest] + 1) % result.shape[longest]] + place[longest + 1:]
    return result.at[tuple(place)].set(smallest).at[tuple(beside)].set(high)


def steps_of(key, extent, cuts, low, largest):
    def one(dim, blocks):
        draws = jax.random.uniform(jax.random.fold_in(jax.random.fold_in(key, 6), dim), (blocks,), jnp.float32, low / len(cuts), largest / len(cuts))
        return jnp.repeat(jnp.exp(draws), extent[dim] // blocks).reshape((-1,) + (1,) * (len(extent) - dim - 1))

    gain = one(*cuts[0])
    for cut in cuts[1:]:
        gain = gain * one(*cut)
    return gain


def gaussian(stream_key, extent, scale, most, cuts=(), kind=jnp.bfloat16):
    result = jax.random.normal(stream_key, extent, jnp.float32) * scale
    if len(cuts) > 0:
        result = steps_of(stream_key, extent, cuts, -0.22, 0.18) * result
    return jnp.clip(result, min=-most, max=most).astype(kind)


def setup_inputs(seed: int = 0) -> dict:
    keys = jax.random.split(jax.random.key(seed), 7)
    return {
        "factor_inv": gaussian(keys[0], (SCEN, SROWS, SROWS), SROWS ** -0.5, 0.21875, ((0, 8),)),
        "pattern": plant((jax.random.randint(keys[1], (SCEN, NBLK, NBLK), 0, 2) < 1).astype(jnp.int32), jax.random.fold_in(keys[1], 1), 0, 1),
        "border": gaussian(keys[2], (SCEN, SROWS, GROUPS * BS), 0.1, 0.59765625, ((0, 8), (2, 4))),
        "row_scale": jnp.clip(jnp.exp(math.log(4.0) - 2.7725887 * jax.random.uniform(keys[3], (SCEN, SROWS), jnp.float32) ** steps_of(keys[3], (SCEN, SROWS), ((0, 8),), -0.2, 0.2)), 0.25, 4.0),
        "link_ids": draw_link_ids(jax.random.fold_in(keys[6], 71), 0),
        "first_diag": jnp.clip(jnp.exp(jax.random.uniform(keys[5], (ORDER,), jnp.float32, math.log(10.0), math.log(100.0))), 10.0, 100.0),
    }


def reference(factor_inv, pattern, border, row_scale, link_ids, first_diag):
    index_blocks = jnp.arange(NBLK)
    diagonal_mask = (index_blocks[:, None] == index_blocks[None, :]).astype(jnp.int32)
    below_diag = (index_blocks[:, None] > index_blocks[None, :]).astype(jnp.int32)

    def add_scenario(schur_sum, inputs):
        finv, pat, bord, scale_rows, link_list = inputs
        effective = jnp.where(diagonal_mask == 1, 1, pat * below_diag)
        expanded = jnp.repeat(jnp.repeat(effective, BS, axis=0), BS, axis=1).astype(jnp.bfloat16)
        masked = finv * expanded
        solved = jnp.dot(masked, bord, preferred_element_type=jnp.float32).astype(jnp.bfloat16)
        scaled = (scale_rows[:, None] * solved.astype(jnp.float32)).astype(jnp.bfloat16)
        schur_block = jnp.dot(scaled.T, solved, preferred_element_type=jnp.float32)
        row_index = (link_list[:, None] * BS + jnp.arange(BS)[None, :]).reshape(-1).astype(jnp.int32)
        schur_sum = schur_sum.at[row_index[:, None], row_index[None, :]].add(schur_block)
        return schur_sum, None

    start_sum = jnp.zeros((ORDER, ORDER), jnp.float32)
    schur_sum = lax.scan(add_scenario, start_sum, (factor_inv, pattern, border, row_scale, link_ids))[0]
    diag_index = jnp.arange(ORDER)
    return schur_sum.at[diag_index, diag_index].add(first_diag)
```

```python
import functools

import jax
import jax.numpy as jnp
from jax import lax
from jax.experimental import pallas as pl
from jax.experimental.pallas import tpu as pltpu
from jax.sharding import PartitionSpec as P


def general_form(factor_inv, pattern, border, row_scale, link_ids, first_diag):
    local_scen, scen_rows, _ = factor_inv.shape
    block_count = pattern.shape[1]
    block_size = border.shape[2]
    order_size = first_diag.shape[0]
    tile_count = lax.axis_size("tile")
    owner_count = lax.axis_size("scen")
    tile_id = lax.axis_index("tile")
    owner_id = lax.axis_index("scen")
    group_blocks = order_size // (tile_count * block_size)
    owner_blocks = order_size // (owner_count * block_size)
    owners_group = owner_count // tile_count
    capacity = local_scen // owners_group + local_scen // (2 * owners_group)
    index_blocks = jnp.arange(block_count)
    diagonal_mask = index_blocks[:, None] == index_blocks[None, :]
    below_diag = (index_blocks[:, None] > index_blocks[None, :]).astype(jnp.int32)
    effective = jnp.where(diagonal_mask[None], 1, pattern * below_diag[None])
    shaped = factor_inv.reshape(local_scen, block_count, block_size, block_count, block_size)
    masked = (shaped * effective[:, :, None, :, None].astype(jnp.bfloat16)).reshape(
        local_scen, scen_rows, scen_rows
    )
    solved_own = jnp.einsum(
        "snm,smc->snc", masked, border, preferred_element_type=jnp.float32
    ).astype(jnp.bfloat16)
    scaled = (row_scale[:, :, None] * solved_own.astype(jnp.float32)).astype(jnp.bfloat16)
    row_blocks = jnp.einsum(
        "snr,snc->src",
        scaled,
        lax.all_gather(solved_own, "tile", axis=2, tiled=True),
        preferred_element_type=jnp.float32,
    )
    blocks_out = jnp.transpose(
        row_blocks.reshape(local_scen, block_size, tile_count, block_size), (0, 2, 1, 3)
    )
    destination = link_ids // owner_blocks
    same_owner = destination[:, None, :] == destination[None, :, :]
    scen_index = jnp.arange(local_scen)
    earlier = (scen_index[None, :] < scen_index[:, None])[:, :, None]
    slot_rank = jnp.sum((same_owner & earlier).astype(jnp.int32), axis=1)
    own_links = lax.dynamic_slice_in_dim(link_ids, tile_id, 1, 1)[:, 0]
    row_local = own_links - tile_id * group_blocks
    target = row_local[:, None] * owner_blocks + link_ids % owner_blocks
    bin_count = group_blocks * owner_blocks
    send_blocks = jnp.zeros((owner_count, capacity, block_size, block_size), jnp.float32)
    send_blocks = send_blocks.at[destination, slot_rank].set(blocks_out)
    send_targets = jnp.full((owner_count, capacity), bin_count, jnp.int32)
    send_targets = send_targets.at[destination, slot_rank].set(target)
    received, received_targets = (
        lax.all_to_all(
            send_blocks.astype(jnp.bfloat16), "scen", split_axis=0, concat_axis=0, tiled=True
        ).astype(send_blocks.dtype),
        lax.all_to_all(send_targets, "scen", split_axis=0, concat_axis=0, tiled=True),
    )
    target_bins = jnp.zeros((bin_count + 1, block_size, block_size), jnp.float32)
    target_bins = target_bins.at[received_targets.reshape(-1)].add(
        received.reshape(-1, block_size, block_size)
    )
    tile_rows = group_blocks * block_size
    tile_cols = owner_blocks * block_size
    tile_out = jnp.transpose(
        target_bins[:bin_count].reshape(group_blocks, owner_blocks, block_size, block_size),
        (0, 2, 1, 3),
    ).reshape(tile_rows, tile_cols)
    row_start = tile_id * tile_rows
    col_start = owner_id * tile_cols
    global_rows = row_start + jnp.arange(tile_rows)
    global_cols = col_start + jnp.arange(tile_cols)
    diag_values = lax.dynamic_slice_in_dim(first_diag, row_start, tile_rows)
    on_diagonal = global_rows[:, None] == global_cols[None, :]
    return tile_out + jnp.where(on_diagonal, diag_values[:, None], 0.0)


MESH = pl.DeviceIdType.MESH
BF16 = jnp.bfloat16
F32 = jnp.float32


def wait_bytes(ref, sem):
    pltpu.make_async_copy(ref, ref, sem).wait()


def loop(count, body):
    def step(i, carry):
        body(i)
        return carry

    lax.fori_loop(0, count, step, 0)


def exchange_kernel(
    nblk, bs, pat_ref, scale_ref, link_ref, factor_ref, border_ref,
    recv_ref, links_ref,
    fbuf, bbuf, own, sib, far, near_out, cross_out,
    f_sem, b_sem, sib_send, sib_recv, far_send, far_recv,
    near_send, cross_send, rcv, fw_send, fw_recv, lk_send, lk_recv,
):
    scen = lax.axis_index("scen")
    tile = lax.axis_index("tile")
    zz, yy = scen // 2, scen % 2
    xx, cc = tile // 2, tile % 2
    xo = 1 - xx
    mate = 2 * xx + 1 - cc

    def ordered(m):
        half, rest = m // 4, m % 4
        chip = lax.rem(xo + half, 2)
        return 2 * chip + rest % 2 + 4 * (rest // 2)

    def load(m):
        s = ordered(m)
        pltpu.make_async_copy(factor_ref.at[s], fbuf.at[s], f_sem.at[s]).start()
        pltpu.make_async_copy(border_ref.at[s], bbuf.at[s], b_sem.at[s]).start()

    loop(8, load)

    barrier = pltpu.get_barrier_semaphore()

    def greet(k):
        place = lax.rem(zz * 4 + tile + k + 1, 16)
        pl.semaphore_signal(
            barrier, inc=1, device_id=(2 * (place // 4) + yy, place % 4), device_id_type=MESH
        )

    def greet_other(k):
        pl.semaphore_signal(
            barrier, inc=1, device_id=(2 * k + 1 - yy, tile), device_id_type=MESH
        )

    loop(15, greet)
    loop(4, greet_other)
    pl.semaphore_wait(barrier, 19)

    def solve(s):
        wait_bytes(fbuf.at[s], f_sem.at[s])
        wait_bytes(bbuf.at[s], b_sem.at[s])
        for a in range(nblk):
            parts = []
            for b in range(a):
                keep = pat_ref[s, a, b].astype(F32)
                block = fbuf[s, a * bs:(a + 1) * bs, b * bs:(b + 1) * bs]
                parts.append((block.astype(F32) * keep).astype(BF16))
            parts.append(fbuf[s, a * bs:(a + 1) * bs, a * bs:(a + 1) * bs])
            left = parts[0] if a == 0 else jnp.concatenate(parts, axis=1)
            out = jnp.dot(left, bbuf[s, :(a + 1) * bs, :], preferred_element_type=F32)
            own[s, a * bs:(a + 1) * bs, :] = out.astype(BF16)

    def to_mate(s):
        return pltpu.make_async_remote_copy(
            own.at[s], sib.at[s], sib_send.at[s], sib_recv.at[s],
            device_id=(scen, mate), device_id_type=MESH,
        )

    def to_far(m):
        s = ordered(m)
        return pltpu.make_async_remote_copy(
            own.at[s], far.at[m // 2, cc], far_send.at[m], far_recv.at[m // 2, cc],
            device_id=(scen, 2 * xo + m % 2), device_id_type=MESH,
        )

    def first(m):
        s = ordered(m)
        solve(s)
        to_far(m).start()
        to_mate(s).start()

    def second(m):
        s = ordered(m + 4)
        solve(s)
        to_mate(s).start()

    def turned(block, s):
        return (block.astype(F32).T * scale_ref[pl.ds(s, 1), :]).astype(BF16)

    def near_copy(half, s):
        column = tile if half == 0 else mate
        return column, pltpu.make_async_remote_copy(
            near_out.at[half, s], recv_ref.at[scen, s], near_send.at[half, s], rcv.at[zz, s],
            device_id=(2 * column + yy, tile), device_id_type=MESH,
        )

    def send_near(half, s):
        column, copy = near_copy(half, s)

        @pl.when(column != zz)
        def _():
            copy.start()

        @pl.when(column == zz)
        def _():
            pltpu.make_async_copy(
                near_out.at[half, s], recv_ref.at[scen, s], rcv.at[zz, s]
            ).start()

    def near(m):
        s = ordered(m)
        wait_bytes(sib.at[s], sib_recv.at[s])
        right = jnp.concatenate([own[s], sib[s]], axis=1)
        out = jnp.dot(turned(own[s], s), right, preferred_element_type=F32).astype(BF16)
        near_out[0, s] = out[:, :bs]
        near_out[1, s] = out[:, bs:]
        send_near(0, s)
        send_near(1, s)

    def cross_copy(k, e):
        s = tile + 4 * k
        if e < 4:
            row = tile if e // 2 == 0 else mate
            column = 2 * xo + e % 2
        else:
            row = 2 * xo + (e - 4) // 2
            column = tile if e % 2 == 0 else mate
        return column, pltpu.make_async_remote_copy(
            cross_out.at[k, e], recv_ref.at[scen, s], cross_send.at[k, e], rcv.at[zz, s],
            device_id=(2 * column + yy, row), device_id_type=MESH,
        )

    def cross(k):
        s = tile + 4 * k
        wait_bytes(far.at[k, 0], far_recv.at[k, 0])
        wait_bytes(far.at[k, 1], far_recv.at[k, 1])
        here = jnp.concatenate([own[s], sib[s]], axis=1)
        there = jnp.concatenate([far[k, 0], far[k, 1]], axis=1)
        for way, (a, b) in enumerate(((here, there), (there, here))):
            out = jnp.dot(turned(a, s), b, preferred_element_type=F32).astype(BF16)
            for e in range(4):
                i, j = e // 2, e % 2
                cross_out[k, 4 * way + e] = out[i * bs:(i + 1) * bs, j * bs:(j + 1) * bs]
        for e in range(7, -1, -1):
            column, copy = cross_copy(k, e)
            if e >= 2:
                copy.start()
            else:

                @pl.when(column != zz)
                def _():
                    copy.start()

                @pl.when(column == zz)
                def _():
                    pltpu.make_async_copy(
                        cross_out.at[k, e], recv_ref.at[scen, s], rcv.at[zz, s]
                    ).start()

    def forward_copy(src, s):
        slot = recv_ref.at[2 * src + yy, s]
        return pltpu.make_async_remote_copy(
            slot, slot, fw_send.at[src, s], fw_recv.at[src, s],
            device_id=(2 * zz + 1 - yy, tile), device_id_type=MESH,
        )

    def forward(base, q):
        s = base + q // 4
        src = lax.rem(zz + q, 4)
        wait_bytes(recv_ref.at[2 * src + yy, s], rcv.at[src, s])
        forward_copy(src, s).start()

    def link_copy(k):
        other = lax.rem(scen + k + 1, 8)
        return other, pltpu.make_async_remote_copy(
            link_ref, links_ref.at[scen], lk_send.at[k], lk_recv.at[scen],
            device_id=(other, tile), device_id_type=MESH,
        )

    loop(4, first)
    loop(4, second)
    loop(8, near)
    pltpu.make_async_copy(link_ref, links_ref.at[scen], lk_recv.at[scen]).start()
    loop(7, lambda k: link_copy(k)[1].start())
    cross(0)
    loop(16, functools.partial(forward, 0))
    cross(1)
    loop(16, functools.partial(forward, 4))

    loop(8, lambda s: wait_bytes(own.at[s], sib_send.at[s]))
    loop(4, lambda m: wait_bytes(own.at[m], far_send.at[m]))

    def sent_near(s):
        for half in range(2):
            column, copy = near_copy(half, s)

            @pl.when(column != zz)
            def _():
                copy.wait_send()

    loop(8, sent_near)
    for k in range(2):
        for e in range(8):
            column, copy = cross_copy(k, e)
            if e >= 2:
                copy.wait_send()
            else:

                @pl.when(column != zz)
                def _():
                    copy.wait_send()

    loop(7, lambda k: link_copy(k)[1].wait_send())
    loop(8, lambda p: wait_bytes(links_ref.at[p], lk_recv.at[p]))

    def finish(q):
        src, s = q % 4, q // 4
        forward_copy(src, s).wait_send()
        wait_bytes(recv_ref.at[2 * src + 1 - yy, s], fw_recv.at[src, s])

    loop(32, finish)


def assemble_kernel(
    group_blocks, owner_blocks, bs, links_ref, recv_ref, diag_ref, out_ref, head, follow, place
):
    scen = lax.axis_index("scen")
    tile = lax.axis_index("tile")
    group = scen * owner_blocks // group_blocks
    r = pl.program_id(0)
    parts, each = recv_ref.shape[0], recv_ref.shape[1]

    @pl.when(r == 0)
    def _():
        def clear(i, carry):
            head[i] = -1
            return carry

        lax.fori_loop(0, group_blocks, clear, 0)

        def enter(n, carry):
            column = links_ref[n // each, n % each, group] - scen * owner_blocks

            @pl.when(jnp.logical_and(column >= 0, column < owner_blocks))
            def _():
                row = links_ref[n // each, n % each, tile] - tile * group_blocks
                follow[n] = head[row]
                place[n] = column
                head[row] = n

            return carry

        lax.fori_loop(0, parts * each, enter, 0)

    out_ref[...] = jnp.zeros_like(out_ref)

    def add(n):
        at = pl.ds(pl.multiple_of(place[n] * bs, bs), bs)
        out_ref[:, at] += recv_ref[n // each, n % each].astype(F32)
        return follow[n]

    lax.while_loop(lambda n: n >= 0, add, head[r])
    block = tile * group_blocks + r
    column = block - scen * owner_blocks

    @pl.when(jnp.logical_and(column >= 0, column < owner_blocks))
    def _():
        at = pl.ds(pl.multiple_of(column * bs, bs), bs)
        values = jnp.broadcast_to(diag_ref[pl.ds(block, 1), :], (bs, bs))
        same = lax.broadcasted_iota(jnp.int32, (bs, bs), 0) == lax.broadcasted_iota(
            jnp.int32, (bs, bs), 1
        )
        out_ref[:, at] += jnp.where(same, values, 0.0)


def two_owner_form(factor_inv, pattern, border, row_scale, link_ids, first_diag):
    local_scen, rows, _ = factor_inv.shape
    nblk = pattern.shape[1]
    bs = border.shape[2]
    order = first_diag.shape[0]
    tiles = lax.axis_size("tile")
    owners = lax.axis_size("scen")
    group_blocks = order // (tiles * bs)
    owner_blocks = order // (owners * bs)
    links = jnp.pad(link_ids, ((0, 0), (0, 128 - link_ids.shape[1])))
    dma = pltpu.SemaphoreType.DMA
    vmem = pl.BlockSpec(memory_space=pltpu.VMEM)
    smem = pl.BlockSpec(memory_space=pltpu.SMEM)
    hbm = pl.BlockSpec(memory_space=pl.ANY)
    received, all_links = pl.pallas_call(
        functools.partial(exchange_kernel, nblk, bs),
        out_shape=(
            jax.ShapeDtypeStruct((owners, local_scen, bs, bs), BF16),
            jax.ShapeDtypeStruct((owners, local_scen, 128), jnp.int32),
        ),
        in_specs=[smem, vmem, vmem, hbm, hbm],
        out_specs=(hbm, hbm),
        scratch_shapes=[
            pltpu.VMEM(factor_inv.shape, BF16),
            pltpu.VMEM(border.shape, BF16),
            pltpu.VMEM((8, rows, bs), BF16),
            pltpu.VMEM((8, rows, bs), BF16),
            pltpu.VMEM((2, 2, rows, bs), BF16),
            pltpu.VMEM((2, 8, bs, bs), BF16),
            pltpu.VMEM((2, 8, bs, bs), BF16),
            dma((8,)), dma((8,)), dma((8,)), dma((8,)), dma((4,)), dma((2, 2)),
            dma((2, 8)), dma((2, 8)), dma((4, 8)), dma((4, 8)), dma((4, 8)),
            dma((7,)), dma((8,)),
        ],
        compiler_params=pltpu.CompilerParams(
            collective_id=0, has_side_effects=True, vmem_limit_bytes=40 * 1024 * 1024
        ),
    )(pattern, row_scale, links, factor_inv, border)
    return pl.pallas_call(
        functools.partial(assemble_kernel, group_blocks, owner_blocks, bs),
        out_shape=jax.ShapeDtypeStruct((group_blocks * bs, owner_blocks * bs), F32),
        grid=(group_blocks,),
        in_specs=[smem, vmem, vmem],
        out_specs=pl.BlockSpec((bs, owner_blocks * bs), lambda r: (r, 0)),
        scratch_shapes=[
            pltpu.SMEM((group_blocks,), jnp.int32),
            pltpu.SMEM((owners * local_scen,), jnp.int32),
            pltpu.SMEM((owners * local_scen,), jnp.int32),
        ],
        compiler_params=pltpu.CompilerParams(vmem_limit_bytes=24 * 1024 * 1024),
    )(all_links, received, first_diag.reshape(order // bs, bs))


def on_device(factor_inv, *rest):
    sizes = (lax.axis_size("tile"), lax.axis_size("scen"), factor_inv.shape[0])
    form = two_owner_form if sizes == (4, 8, 8) else general_form
    return form(factor_inv, *rest)


def solution(mesh):
    in_specs = (
        P("scen", None, None),
        P("scen", None, None),
        P("scen", None, "tile"),
        P("scen", None),
        P("scen", None),
        P(),
    )
    out_specs = P("tile", "scen")
    return jax.shard_map(
        on_device, mesh=mesh, in_specs=in_specs, out_specs=out_specs, check_vma=False
    )
```

```python
import functools

import jax
import jax.numpy as jnp
from jax import lax
from jax.experimental import pallas as pl
from jax.experimental.pallas import tpu as pltpu
from jax.sharding import PartitionSpec as P


def general_form(factor_inv, pattern, border, row_scale, link_ids, first_diag):
    local_scen, scen_rows, _ = factor_inv.shape
    block_count = pattern.shape[1]
    block_size = border.shape[2]
    order_size = first_diag.shape[0]
    tile_count = lax.axis_size("tile")
    owner_count = lax.axis_size("scen")
    tile_id = lax.axis_index("tile")
    owner_id = lax.axis_index("scen")
    group_blocks = order_size // (tile_count * block_size)
    owner_blocks = order_size // (owner_count * block_size)
    owners_group = owner_count // tile_count
    capacity = local_scen // owners_group + local_scen // (2 * owners_group)
    index_blocks = jnp.arange(block_count)
    diagonal_mask = index_blocks[:, None] == index_blocks[None, :]
    below_diag = (index_blocks[:, None] > index_blocks[None, :]).astype(jnp.int32)
    effective = jnp.where(diagonal_mask[None], 1, pattern * below_diag[None])
    shaped = factor_inv.reshape(local_scen, block_count, block_size, block_count, block_size)
    masked = (shaped * effective[:, :, None, :, None].astype(jnp.bfloat16)).reshape(
        local_scen, scen_rows, scen_rows
    )
    solved_own = jnp.einsum(
        "snm,smc->snc", masked, border, preferred_element_type=jnp.float32
    ).astype(jnp.bfloat16)
    scaled = (row_scale[:, :, None] * solved_own.astype(jnp.float32)).astype(jnp.bfloat16)
    row_blocks = jnp.einsum(
        "snr,snc->src",
        scaled,
        lax.all_gather(solved_own, "tile", axis=2, tiled=True),
        preferred_element_type=jnp.float32,
    )
    blocks_out = jnp.transpose(
        row_blocks.reshape(local_scen, block_size, tile_count, block_size), (0, 2, 1, 3)
    )
    destination = link_ids // owner_blocks
    same_owner = destination[:, None, :] == destination[None, :, :]
    scen_index = jnp.arange(local_scen)
    earlier = (scen_index[None, :] < scen_index[:, None])[:, :, None]
    slot_rank = jnp.sum((same_owner & earlier).astype(jnp.int32), axis=1)
    own_links = lax.dynamic_slice_in_dim(link_ids, tile_id, 1, 1)[:, 0]
    row_local = own_links - tile_id * group_blocks
    target = row_local[:, None] * owner_blocks + link_ids % owner_blocks
    bin_count = group_blocks * owner_blocks
    send_blocks = jnp.zeros((owner_count, capacity, block_size, block_size), jnp.float32)
    send_blocks = send_blocks.at[destination, slot_rank].set(blocks_out)
    send_targets = jnp.full((owner_count, capacity), bin_count, jnp.int32)
    send_targets = send_targets.at[destination, slot_rank].set(target)
    received, received_targets = (
        lax.all_to_all(
            send_blocks.astype(jnp.bfloat16), "scen", split_axis=0, concat_axis=0, tiled=True
        ).astype(send_blocks.dtype),
        lax.all_to_all(send_targets, "scen", split_axis=0, concat_axis=0, tiled=True),
    )
    target_bins = jnp.zeros((bin_count + 1, block_size, block_size), jnp.float32)
    target_bins = target_bins.at[received_targets.reshape(-1)].add(
        received.reshape(-1, block_size, block_size)
    )
    tile_rows = group_blocks * block_size
    tile_cols = owner_blocks * block_size
    tile_out = jnp.transpose(
        target_bins[:bin_count].reshape(group_blocks, owner_blocks, block_size, block_size),
        (0, 2, 1, 3),
    ).reshape(tile_rows, tile_cols)
    row_start = tile_id * tile_rows
    col_start = owner_id * tile_cols
    global_rows = row_start + jnp.arange(tile_rows)
    global_cols = col_start + jnp.arange(tile_cols)
    diag_values = lax.dynamic_slice_in_dim(first_diag, row_start, tile_rows)
    on_diagonal = global_rows[:, None] == global_cols[None, :]
    return tile_out + jnp.where(on_diagonal, diag_values[:, None], 0.0)


MESH = pl.DeviceIdType.MESH
BF16 = jnp.bfloat16
F32 = jnp.float32


def wait_bytes(ref, sem):
    pltpu.make_async_copy(ref, ref, sem).wait()


def loop(count, body):
    def step(i, carry):
        body(i)
        return carry

    lax.fori_loop(0, count, step, 0)


def exchange_kernel(
    nblk, bs, pat_ref, scale_ref, link_ref, factor_ref, border_ref,
    recv_ref, links_ref,
    fbuf, bbuf, own, sib, far, near_out, cross_out,
    f_sem, b_sem, sib_send, sib_recv, far_send, far_recv,
    near_send, cross_send, rcv, fw_send, fw_recv, lk_send, lk_recv,
):
    scen = lax.axis_index("scen")
    tile = lax.axis_index("tile")
    zz, yy = scen // 2, scen % 2
    xx, cc = tile // 2, tile % 2
    xo = 1 - xx
    mate = 2 * xx + 1 - cc

    def ordered(m):
        half, rest = m // 4, m % 4
        chip = lax.rem(xo + half, 2)
        return 2 * chip + rest % 2 + 4 * (rest // 2)

    def load(m):
        s = ordered(m)
        pltpu.make_async_copy(factor_ref.at[s], fbuf.at[s], f_sem.at[s]).start()
        pltpu.make_async_copy(border_ref.at[s], bbuf.at[s], b_sem.at[s]).start()

    loop(8, load)

    barrier = pltpu.get_barrier_semaphore()

    def greet(k):
        place = lax.rem(zz * 4 + tile + k + 1, 16)
        pl.semaphore_signal(
            barrier, inc=1, device_id=(2 * (place // 4) + yy, place % 4), device_id_type=MESH
        )

    def greet_other(k):
        pl.semaphore_signal(
            barrier, inc=1, device_id=(2 * k + 1 - yy, tile), device_id_type=MESH
        )

    loop(15, greet)
    loop(4, greet_other)
    pl.semaphore_wait(barrier, 19)

    def solve(s):
        wait_bytes(fbuf.at[s], f_sem.at[s])
        wait_bytes(bbuf.at[s], b_sem.at[s])
        total = None
        for first_col in range(0, nblk, 2):
            lines = []
            for a in range(first_col, nblk):
                parts = []
                for b in range(first_col, first_col + 2):
                    block = fbuf[s, a * bs:(a + 1) * bs, b * bs:(b + 1) * bs]
                    if b < a:
                        keep = pat_ref[a, s, b].astype(F32)
                        block = (block.astype(F32) * keep).astype(BF16)
                    elif b > a:
                        block = jnp.zeros((bs, bs), BF16)
                    parts.append(block)
                lines.append(jnp.concatenate(parts, axis=1))
            right = bbuf[s, first_col * bs:(first_col + 2) * bs, :]
            out = jnp.dot(jnp.concatenate(lines, axis=0), right, preferred_element_type=F32)
            if total is not None:
                out = out + total[2 * bs:]
            own[s, first_col * bs:(first_col + 2) * bs, :] = out[:2 * bs].astype(BF16)
            total = out

    def to_mate(s):
        return pltpu.make_async_remote_copy(
            own.at[s], sib.at[s], sib_send.at[s], sib_recv.at[s],
            device_id=(scen, mate), device_id_type=MESH,
        )

    def to_far(m):
        s = ordered(m)
        return pltpu.make_async_remote_copy(
            own.at[s], far.at[m // 2, cc], far_send.at[m], far_recv.at[m // 2, cc],
            device_id=(scen, 2 * xo + m % 2), device_id_type=MESH,
        )

    def first(k):
        for m in (2 * k, 2 * k + 1):
            solve(ordered(m))
            to_far(m).start()
            to_mate(ordered(m)).start()

    def second(k):
        for m in (2 * k + 4, 2 * k + 5):
            solve(ordered(m))
            to_mate(ordered(m)).start()

    def turned(block, s):
        return (block.T.astype(F32) * scale_ref[pl.ds(s, 1), :]).astype(BF16)

    def near_copy(half, p):
        column = tile if half == 0 else mate
        two = pl.ds(2 * p, 2)
        return column, pltpu.make_async_remote_copy(
            near_out.at[half, two], recv_ref.at[scen, two], near_send.at[half, p], rcv.at[zz, p],
            device_id=(2 * column + yy, tile), device_id_type=MESH,
        )

    def near(h):
        p = lax.rem(xo + h // 2, 2) + 2 * (h % 2)
        for s in (2 * p, 2 * p + 1):
            wait_bytes(sib.at[s], sib_recv.at[s])
            right = jnp.concatenate([own[s], sib[s]], axis=1)
            out = jnp.dot(turned(own[s], s), right, preferred_element_type=F32).astype(BF16)
            near_out[0, s] = out[:, :bs]
            near_out[1, s] = out[:, bs:]
        for half in range(2):
            column, copy = near_copy(half, p)

            @pl.when(column != zz)
            def _():
                copy.start()

            @pl.when(column == zz)
            def _():
                two = pl.ds(2 * p, 2)
                pltpu.make_async_copy(
                    near_out.at[half, two], recv_ref.at[scen, two], rcv.at[zz, p]
                ).start()

    def cross_copy(k, e):
        s = tile + 4 * k
        if e < 4:
            row = tile if e // 2 == 0 else mate
            column = 2 * xo + e % 2
        else:
            row = 2 * xo + (e - 4) // 2
            column = tile if e % 2 == 0 else mate
        return column, pltpu.make_async_remote_copy(
            cross_out.at[k, e], recv_ref.at[scen, s], cross_send.at[k, e], rcv.at[zz, 2 * k + tile // 2],
            device_id=(2 * column + yy, row), device_id_type=MESH,
        )

    def cross(k):
        s = tile + 4 * k
        wait_bytes(far.at[k, 0], far_recv.at[k, 0])
        wait_bytes(far.at[k, 1], far_recv.at[k, 1])
        here = jnp.concatenate([own[s], sib[s]], axis=1)
        there = jnp.concatenate([far[k, 0], far[k, 1]], axis=1)
        for way, (a, b) in enumerate(((here, there), (there, here))):
            out = jnp.dot(turned(a, s), b, preferred_element_type=F32).astype(BF16)
            for e in range(4):
                i, j = e // 2, e % 2
                cross_out[k, 4 * way + e] = out[i * bs:(i + 1) * bs, j * bs:(j + 1) * bs]
        for e in range(7, -1, -1):
            column, copy = cross_copy(k, e)
            if e >= 2:
                copy.start()
            else:

                @pl.when(column != zz)
                def _():
                    copy.start()

                @pl.when(column == zz)
                def _():
                    pltpu.make_async_copy(
                        cross_out.at[k, e], recv_ref.at[scen, s], rcv.at[zz, 2 * k + tile // 2]
                    ).start()

    def forward_copy(src, p):
        slot = recv_ref.at[2 * src + yy, pl.ds(2 * p, 2)]
        return pltpu.make_async_remote_copy(
            slot, slot, fw_send.at[src, p], fw_recv.at[src, p],
            device_id=(2 * zz + 1 - yy, tile), device_id_type=MESH,
        )

    def forward(near_type, part, q):
        if near_type:
            p = lax.rem(xo + part, 2) + 2 * (q // 4)
        else:
            p = 2 * part + q // 4
        src = lax.rem(zz + q, 4)
        wait_bytes(recv_ref.at[2 * src + yy, pl.ds(2 * p, 2)], rcv.at[src, p])
        forward_copy(src, p).start()

    def link_copy(k):
        other = lax.rem(scen + k + 1, 8)
        return other, pltpu.make_async_remote_copy(
            link_ref, links_ref.at[scen], lk_send.at[k], lk_recv.at[scen],
            device_id=(other, tile), device_id_type=MESH,
        )

    loop(2, first)
    loop(2, near)
    loop(2, second)
    loop(2, lambda h: near(h + 2))

    @pl.when(zz // 2 == xx)
    def _():
        loop(8, functools.partial(forward, True, 0))

    cross(0)

    @pl.when(zz // 2 == xx)
    def _():
        loop(8, functools.partial(forward, True, 1))

    @pl.when(zz // 2 != xx)
    def _():
        loop(8, functools.partial(forward, False, 0))

    cross(1)
    pltpu.make_async_copy(link_ref, links_ref.at[scen], lk_recv.at[scen]).start()
    loop(7, lambda k: link_copy(k)[1].start())

    @pl.when(zz // 2 != xx)
    def _():
        loop(8, functools.partial(forward, False, 1))

    loop(8, lambda s: wait_bytes(own.at[s], sib_send.at[s]))
    loop(4, lambda m: wait_bytes(own.at[m], far_send.at[m]))

    def sent_near(p):
        for half in range(2):
            column, copy = near_copy(half, p)

            @pl.when(column != zz)
            def _():
                copy.wait_send()

    loop(4, sent_near)
    for k in range(2):
        for e in range(8):
            column, copy = cross_copy(k, e)
            if e >= 2:
                copy.wait_send()
            else:

                @pl.when(column != zz)
                def _():
                    copy.wait_send()

    loop(7, lambda k: link_copy(k)[1].wait_send())
    loop(8, lambda p: wait_bytes(links_ref.at[p], lk_recv.at[p]))

    def finish(q):
        src, p = q % 4, q // 4
        forward_copy(src, p).wait_send()
        wait_bytes(recv_ref.at[2 * src + 1 - yy, pl.ds(2 * p, 2)], fw_recv.at[src, p])

    loop(16, finish)


def assemble_kernel(
    group_blocks, owner_blocks, bs, links_ref, recv_ref, diag_ref, out_ref, head, follow, place
):
    scen = lax.axis_index("scen")
    tile = lax.axis_index("tile")
    group = scen * owner_blocks // group_blocks
    first = pl.program_id(0) * (out_ref.shape[0] // bs)
    parts, each = recv_ref.shape[0], recv_ref.shape[1]

    @pl.when(first == 0)
    def _():
        for i in range(group_blocks):
            head[i] = -1

        def enter(p, carry):
            for s in range(each):
                column = links_ref[p, group, s] - scen * owner_blocks
                n = p * each + s

                @pl.when(jnp.logical_and(column >= 0, column < owner_blocks))
                def _():
                    row = links_ref[p, tile, s] - tile * group_blocks
                    follow[n] = head[row]
                    place[n] = column
                    head[row] = n

            return carry

        lax.fori_loop(0, parts, enter, 0)

    out_ref[...] = jnp.zeros_like(out_ref)
    same = lax.broadcasted_iota(jnp.int32, (bs, bs), 0) == lax.broadcasted_iota(
        jnp.int32, (bs, bs), 1
    )
    for i in range(out_ref.shape[0] // bs):
        rows = slice(i * bs, (i + 1) * bs)

        def add(n):
            at = pl.ds(pl.multiple_of(place[n] * bs, bs), bs)
            out_ref[rows, at] += recv_ref[n // each, n % each].astype(F32)
            return follow[n]

        lax.while_loop(lambda n: n >= 0, add, head[first + i])
        block = tile * group_blocks + first + i
        column = block - scen * owner_blocks

        @pl.when(jnp.logical_and(column >= 0, column < owner_blocks))
        def _():
            at = pl.ds(pl.multiple_of(column * bs, bs), bs)
            values = jnp.broadcast_to(diag_ref[pl.ds(block, 1), :], (bs, bs))
            out_ref[rows, at] += jnp.where(same, values, 0.0)


def two_owner_form(factor_inv, pattern, border, row_scale, link_ids, first_diag):
    local_scen, rows, _ = factor_inv.shape
    nblk = pattern.shape[1]
    bs = border.shape[2]
    order = first_diag.shape[0]
    tiles = lax.axis_size("tile")
    owners = lax.axis_size("scen")
    group_blocks = order // (tiles * bs)
    owner_blocks = order // (owners * bs)
    links = jnp.pad(link_ids.T, ((0, 8 - link_ids.shape[1]), (0, 128 - local_scen)))
    dma = pltpu.SemaphoreType.DMA
    vmem = pl.BlockSpec(memory_space=pltpu.VMEM)
    smem = pl.BlockSpec(memory_space=pltpu.SMEM)
    hbm = pl.BlockSpec(memory_space=pl.ANY)
    received, all_links = pl.pallas_call(
        functools.partial(exchange_kernel, nblk, bs),
        out_shape=(
            jax.ShapeDtypeStruct((owners, local_scen, bs, bs), BF16),
            jax.ShapeDtypeStruct((owners, 8, 128), jnp.int32),
        ),
        in_specs=[smem, vmem, vmem, hbm, hbm],
        out_specs=(hbm, hbm),
        scratch_shapes=[
            pltpu.VMEM(factor_inv.shape, BF16),
            pltpu.VMEM(border.shape, BF16),
            pltpu.VMEM((8, rows, bs), BF16),
            pltpu.VMEM((8, rows, bs), BF16),
            pltpu.VMEM((2, 2, rows, bs), BF16),
            pltpu.VMEM((2, 8, bs, bs), BF16),
            pltpu.VMEM((2, 8, bs, bs), BF16),
            dma((8,)), dma((8,)), dma((8,)), dma((8,)), dma((4,)), dma((2, 2)),
            dma((2, 4)), dma((2, 8)), dma((4, 4)), dma((4, 4)), dma((4, 4)),
            dma((7,)), dma((8,)),
        ],
        compiler_params=pltpu.CompilerParams(
            collective_id=0, has_side_effects=True, vmem_limit_bytes=62 * 1024 * 1024
        ),
    )(jnp.transpose(pattern, (1, 0, 2)), row_scale, links, factor_inv, border)
    return pl.pallas_call(
        functools.partial(assemble_kernel, group_blocks, owner_blocks, bs),
        out_shape=jax.ShapeDtypeStruct((group_blocks * bs, owner_blocks * bs), F32),
        grid=(group_blocks // 4,),
        in_specs=[smem, vmem, vmem],
        out_specs=pl.BlockSpec((4 * bs, owner_blocks * bs), lambda r: (r, 0)),
        scratch_shapes=[
            pltpu.SMEM((group_blocks,), jnp.int32),
            pltpu.SMEM((owners * local_scen,), jnp.int32),
            pltpu.SMEM((owners * local_scen,), jnp.int32),
        ],
        compiler_params=pltpu.CompilerParams(vmem_limit_bytes=24 * 1024 * 1024),
    )(all_links, received, first_diag.reshape(order // bs, bs))


def on_device(factor_inv, *rest):
    sizes = (lax.axis_size("tile"), lax.axis_size("scen"), factor_inv.shape[0])
    form = two_owner_form if sizes == (4, 8, 8) else general_form
    return form(factor_inv, *rest)


def solution(mesh):
    in_specs = (
        P("scen", None, None),
        P("scen", None, None),
        P("scen", None, "tile"),
        P("scen", None),
        P("scen", None),
        P(),
    )
    out_specs = P("tile", "scen")
    return jax.shard_map(
        on_device, mesh=mesh, in_specs=in_specs, out_specs=out_specs, check_vma=False
    )
```

```python
import functools

import jax
import jax.numpy as jnp
from jax import lax
from jax.experimental import pallas as pl
from jax.experimental.pallas import tpu as pltpu
from jax.sharding import PartitionSpec as P


def general_form(factor_inv, pattern, border, row_scale, link_ids, first_diag):
    local_scen, scen_rows, _ = factor_inv.shape
    block_count = pattern.shape[1]
    block_size = border.shape[2]
    order_size = first_diag.shape[0]
    tile_count = lax.axis_size("tile")
    owner_count = lax.axis_size("scen")
    tile_id = lax.axis_index("tile")
    owner_id = lax.axis_index("scen")
    group_blocks = order_size // (tile_count * block_size)
    owner_blocks = order_size // (owner_count * block_size)
    owners_group = owner_count // tile_count
    capacity = local_scen // owners_group + local_scen // (2 * owners_group)
    index_blocks = jnp.arange(block_count)
    diagonal_mask = index_blocks[:, None] == index_blocks[None, :]
    below_diag = (index_blocks[:, None] > index_blocks[None, :]).astype(jnp.int32)
    effective = jnp.where(diagonal_mask[None], 1, pattern * below_diag[None])
    shaped = factor_inv.reshape(local_scen, block_count, block_size, block_count, block_size)
    masked = (shaped * effective[:, :, None, :, None].astype(jnp.bfloat16)).reshape(
        local_scen, scen_rows, scen_rows
    )
    solved_own = jnp.einsum(
        "snm,smc->snc", masked, border, preferred_element_type=jnp.float32
    ).astype(jnp.bfloat16)
    scaled = (row_scale[:, :, None] * solved_own.astype(jnp.float32)).astype(jnp.bfloat16)
    row_blocks = jnp.einsum(
        "snr,snc->src",
        scaled,
        lax.all_gather(solved_own, "tile", axis=2, tiled=True),
        preferred_element_type=jnp.float32,
    )
    blocks_out = jnp.transpose(
        row_blocks.reshape(local_scen, block_size, tile_count, block_size), (0, 2, 1, 3)
    )
    destination = link_ids // owner_blocks
    same_owner = destination[:, None, :] == destination[None, :, :]
    scen_index = jnp.arange(local_scen)
    earlier = (scen_index[None, :] < scen_index[:, None])[:, :, None]
    slot_rank = jnp.sum((same_owner & earlier).astype(jnp.int32), axis=1)
    own_links = lax.dynamic_slice_in_dim(link_ids, tile_id, 1, 1)[:, 0]
    row_local = own_links - tile_id * group_blocks
    target = row_local[:, None] * owner_blocks + link_ids % owner_blocks
    bin_count = group_blocks * owner_blocks
    send_blocks = jnp.zeros((owner_count, capacity, block_size, block_size), jnp.float32)
    send_blocks = send_blocks.at[destination, slot_rank].set(blocks_out)
    send_targets = jnp.full((owner_count, capacity), bin_count, jnp.int32)
    send_targets = send_targets.at[destination, slot_rank].set(target)
    received, received_targets = (
        lax.all_to_all(
            send_blocks.astype(jnp.bfloat16), "scen", split_axis=0, concat_axis=0, tiled=True
        ).astype(send_blocks.dtype),
        lax.all_to_all(send_targets, "scen", split_axis=0, concat_axis=0, tiled=True),
    )
    target_bins = jnp.zeros((bin_count + 1, block_size, block_size), jnp.float32)
    target_bins = target_bins.at[received_targets.reshape(-1)].add(
        received.reshape(-1, block_size, block_size)
    )
    tile_rows = group_blocks * block_size
    tile_cols = owner_blocks * block_size
    tile_out = jnp.transpose(
        target_bins[:bin_count].reshape(group_blocks, owner_blocks, block_size, block_size),
        (0, 2, 1, 3),
    ).reshape(tile_rows, tile_cols)
    row_start = tile_id * tile_rows
    col_start = owner_id * tile_cols
    global_rows = row_start + jnp.arange(tile_rows)
    global_cols = col_start + jnp.arange(tile_cols)
    diag_values = lax.dynamic_slice_in_dim(first_diag, row_start, tile_rows)
    on_diagonal = global_rows[:, None] == global_cols[None, :]
    return tile_out + jnp.where(on_diagonal, diag_values[:, None], 0.0)


MESH = pl.DeviceIdType.MESH
BF16 = jnp.bfloat16
F32 = jnp.float32


def wait_bytes(ref, sem):
    pltpu.make_async_copy(ref, ref, sem).wait()


def loop(count, body):
    def step(i, carry):
        body(i)
        return carry

    lax.fori_loop(0, count, step, 0)


def exchange_kernel(
    nblk, bs, pat_ref, scale_ref, link_ref, factor_ref, border_ref,
    recv_ref, links_ref,
    fbuf, bbuf, own, sib, far, near_out, cross_out, lbuf,
    f_sem, b_sem, sib_send, sib_recv, far_send, far_recv,
    near_send, cross_send, both_send, rcv, fw_send, fw_recv, lk_send, lk_recv,
):
    scen = lax.axis_index("scen")
    tile = lax.axis_index("tile")
    zz, yy = scen // 2, scen % 2
    xx, cc = tile // 2, tile % 2
    xo = 1 - xx
    mate = 2 * xx + 1 - cc

    def ordered(m):
        half, rest = m // 4, m % 4
        chip = lax.rem(xo + half, 2)
        return 2 * chip + rest % 2 + 4 * (rest // 2)

    def load(m):
        s = ordered(m)
        pltpu.make_async_copy(factor_ref.at[s], fbuf.at[s], f_sem.at[s]).start()
        pltpu.make_async_copy(border_ref.at[s], bbuf.at[s], b_sem.at[s]).start()

    loop(8, load)

    barrier = pltpu.get_barrier_semaphore()

    def greet(k):
        place = lax.rem(scen * 4 + tile + k + 1, 32)
        pl.semaphore_signal(
            barrier, inc=1, device_id=(place // 4, place % 4), device_id_type=MESH
        )

    loop(31, greet)
    pl.semaphore_wait(barrier, 31)

    def solve(s):
        wait_bytes(fbuf.at[s], f_sem.at[s])
        wait_bytes(bbuf.at[s], b_sem.at[s])
        total = None
        for first_col in range(0, nblk, 2):
            lines = []
            for a in range(first_col, nblk):
                parts = []
                for b in range(first_col, first_col + 2):
                    block = fbuf[s, a * bs:(a + 1) * bs, b * bs:(b + 1) * bs]
                    if b < a:
                        keep = pat_ref[a, s, b].astype(F32)
                        block = (block.astype(F32) * keep).astype(BF16)
                    elif b > a:
                        block = jnp.zeros((bs, bs), BF16)
                    parts.append(block)
                lines.append(jnp.concatenate(parts, axis=1))
            right = bbuf[s, first_col * bs:(first_col + 2) * bs, :]
            out = jnp.dot(jnp.concatenate(lines, axis=0), right, preferred_element_type=F32)
            if total is not None:
                out = out + total[2 * bs:]
            own[s, first_col * bs:(first_col + 2) * bs, :] = out[:2 * bs].astype(BF16)
            total = out

    def to_mate(s):
        return pltpu.make_async_remote_copy(
            own.at[s], sib.at[s], sib_send.at[s], sib_recv.at[s],
            device_id=(scen, mate), device_id_type=MESH,
        )

    def to_far(m):
        s = ordered(m)
        return pltpu.make_async_remote_copy(
            own.at[s], far.at[m // 2, cc], far_send.at[m], far_recv.at[m // 2, cc],
            device_id=(scen, 2 * xo + m % 2), device_id_type=MESH,
        )

    def first(k):
        for m in (2 * k, 2 * k + 1):
            solve(ordered(m))
            to_far(m).start()
            to_mate(ordered(m)).start()

    def second(k):
        for m in (2 * k + 4, 2 * k + 5):
            solve(ordered(m))
            to_mate(ordered(m)).start()

    def turned(block, s):
        return (block.T.astype(F32) * scale_ref[pl.ds(s, 1), :]).astype(BF16)

    def near_copy(half, p):
        column = tile if half == 0 else mate
        two = pl.ds(2 * p, 2)
        return column, pltpu.make_async_remote_copy(
            near_out.at[half, two], recv_ref.at[scen, two], near_send.at[half, p], rcv.at[zz, p],
            device_id=(2 * column + yy, tile), device_id_type=MESH,
        )

    def near(h):
        p = lax.rem(xo + h // 2, 2) + 2 * (h % 2)
        for s in (2 * p, 2 * p + 1):
            wait_bytes(sib.at[s], sib_recv.at[s])
            right = jnp.concatenate([own[s], sib[s]], axis=1)
            out = jnp.dot(turned(own[s], s), right, preferred_element_type=F32).astype(BF16)
            near_out[0, s] = out[:, :bs]
            near_out[1, s] = out[:, bs:]
        for half in range(2):
            column, copy = near_copy(half, p)

            @pl.when(column != zz)
            def _():
                copy.start()

            @pl.when(column == zz)
            def _():
                two = pl.ds(2 * p, 2)
                pltpu.make_async_copy(
                    near_out.at[half, two], recv_ref.at[scen, two], rcv.at[zz, p]
                ).start()

    def cross_copy(k, e, other=False):
        s = tile + 4 * k
        if e < 4:
            row = tile if e // 2 == 0 else mate
            column = 2 * xo + e % 2
        else:
            row = 2 * xo + (e - 4) // 2
            column = tile if e % 2 == 0 else mate
        y = 1 - yy if other else yy
        got = (fw_recv if other else rcv).at[zz, 2 * k + tile // 2]
        gone = both_send.at[e] if other else cross_send.at[k, e]
        return column, pltpu.make_async_remote_copy(
            cross_out.at[k, e], recv_ref.at[scen, s], gone, got,
            device_id=(2 * column + y, row), device_id_type=MESH,
        )

    def cross(k):
        s = tile + 4 * k
        wait_bytes(far.at[k, 0], far_recv.at[k, 0])
        wait_bytes(far.at[k, 1], far_recv.at[k, 1])
        here = jnp.concatenate([own[s], sib[s]], axis=1)
        there = jnp.concatenate([far[k, 0], far[k, 1]], axis=1)
        for way, (a, b) in enumerate(((here, there), (there, here))):
            out = jnp.dot(turned(a, s), b, preferred_element_type=F32).astype(BF16)
            for e in range(4):
                i, j = e // 2, e % 2
                cross_out[k, 4 * way + e] = out[i * bs:(i + 1) * bs, j * bs:(j + 1) * bs]
        for e in range(7, -1, -1):
            column, copy = cross_copy(k, e)
            if k == 1:
                cross_copy(k, e, True)[1].start()
            if e >= 2:
                copy.start()
            else:

                @pl.when(column != zz)
                def _():
                    copy.start()

                @pl.when(column == zz)
                def _():
                    pltpu.make_async_copy(
                        cross_out.at[k, e], recv_ref.at[scen, s], rcv.at[zz, 2 * k + tile // 2]
                    ).start()

    def forward_copy(src, p):
        slot = recv_ref.at[2 * src + yy, pl.ds(2 * p, 2)]
        return pltpu.make_async_remote_copy(
            slot, slot, fw_send.at[src, p], fw_recv.at[src, p],
            device_id=(2 * zz + 1 - yy, tile), device_id_type=MESH,
        )

    def forward(near_type, part, q):
        if near_type:
            p = lax.rem(xo + part, 2) + 2 * (q // 4)
        else:
            p = q // 4
        src = lax.rem(zz + q, 4)
        wait_bytes(recv_ref.at[2 * src + yy, pl.ds(2 * p, 2)], rcv.at[src, p])
        forward_copy(src, p).start()

    def link_copy(k):
        other = lax.rem(scen + k + 1, 8)
        return other, pltpu.make_async_remote_copy(
            lbuf, links_ref.at[scen], lk_send.at[k], lk_recv.at[scen],
            device_id=(other, tile), device_id_type=MESH,
        )

    loop(2, first)
    loop(2, near)
    loop(2, second)
    loop(2, lambda h: near(h + 2))

    cross(0)

    @pl.when(zz // 2 == xx)
    def _():
        loop(8, functools.partial(forward, True, 0))

    @pl.when(zz // 2 != xx)
    def _():
        loop(8, functools.partial(forward, False, 0))

    cross(1)

    @pl.when(zz // 2 == xx)
    def _():
        loop(8, functools.partial(forward, True, 1))

    lbuf[...] = jnp.zeros_like(lbuf)
    lbuf[:link_ref.shape[0], :link_ref.shape[1]] = link_ref[...]
    pltpu.make_async_copy(lbuf, links_ref.at[scen], lk_recv.at[scen]).start()
    loop(7, lambda k: link_copy(k)[1].start())

    loop(8, lambda s: wait_bytes(own.at[s], sib_send.at[s]))
    loop(4, lambda m: wait_bytes(own.at[m], far_send.at[m]))

    def sent_near(p):
        for half in range(2):
            column, copy = near_copy(half, p)

            @pl.when(column != zz)
            def _():
                copy.wait_send()

    loop(4, sent_near)
    for k in range(2):
        for e in range(8):
            column, copy = cross_copy(k, e)
            if e >= 2:
                copy.wait_send()
            else:

                @pl.when(column != zz)
                def _():
                    copy.wait_send()

    for e in range(8):
        cross_copy(1, e, True)[1].wait_send()
    loop(7, lambda k: link_copy(k)[1].wait_send())
    loop(8, lambda p: wait_bytes(links_ref.at[p], lk_recv.at[p]))

    def forwarded(q):
        forward_copy(q % 4, q // 4).wait_send()

    def arrived(q):
        src, p = q % 4, q // 4 + 2
        wait_bytes(recv_ref.at[2 * src + yy, pl.ds(2 * p, 2)], rcv.at[src, p])

    def arrived_other(q):
        src, p = q % 4, q // 4
        wait_bytes(recv_ref.at[2 * src + 1 - yy, pl.ds(2 * p, 2)], fw_recv.at[src, p])

    @pl.when(zz // 2 == xx)
    def _():
        loop(16, forwarded)

    @pl.when(zz // 2 != xx)
    def _():
        loop(8, forwarded)
        loop(8, arrived)

    loop(16, arrived_other)


def assemble_kernel(
    group_blocks, owner_blocks, bs, links_ref, recv_ref, diag_ref, out_ref,
    blocks, head, follow, place, sem,
):
    scen = lax.axis_index("scen")
    tile = lax.axis_index("tile")
    group = scen * owner_blocks // group_blocks
    first = pl.program_id(0) * (out_ref.shape[0] // bs)
    parts, each = recv_ref.shape[0], recv_ref.shape[1]

    @pl.when(first == 0)
    def _():
        copy = pltpu.make_async_copy(recv_ref, blocks, sem)
        copy.start()
        for i in range(group_blocks):
            head[i] = -1

        def enter(p, carry):
            for s in range(each):
                column = links_ref[p, group, s] - scen * owner_blocks
                n = p * each + s

                @pl.when(jnp.logical_and(column >= 0, column < owner_blocks))
                def _():
                    row = links_ref[p, tile, s] - tile * group_blocks
                    follow[n] = head[row]
                    place[n] = column
                    head[row] = n

            return carry

        lax.fori_loop(0, parts, enter, 0)
        copy.wait()

    out_ref[...] = jnp.zeros_like(out_ref)
    same = lax.broadcasted_iota(jnp.int32, (bs, bs), 0) == lax.broadcasted_iota(
        jnp.int32, (bs, bs), 1
    )
    for i in range(out_ref.shape[0] // bs):
        rows = slice(i * bs, (i + 1) * bs)

        def add(n):
            at = pl.ds(pl.multiple_of(place[n] * bs, bs), bs)
            out_ref[rows, at] += blocks[n // each, n % each].astype(F32)
            return follow[n]

        lax.while_loop(lambda n: n >= 0, add, head[first + i])
        block = tile * group_blocks + first + i
        column = block - scen * owner_blocks

        @pl.when(jnp.logical_and(column >= 0, column < owner_blocks))
        def _():
            at = pl.ds(pl.multiple_of(column * bs, bs), bs)
            values = jnp.broadcast_to(diag_ref[pl.ds(block, 1), :], (bs, bs))
            out_ref[rows, at] += jnp.where(same, values, 0.0)


def two_owner_form(factor_inv, pattern, border, row_scale, link_ids, first_diag):
    local_scen, rows, _ = factor_inv.shape
    nblk = pattern.shape[1]
    bs = border.shape[2]
    order = first_diag.shape[0]
    tiles = lax.axis_size("tile")
    owners = lax.axis_size("scen")
    group_blocks = order // (tiles * bs)
    owner_blocks = order // (owners * bs)
    dma = pltpu.SemaphoreType.DMA
    vmem = pl.BlockSpec(memory_space=pltpu.VMEM)
    smem = pl.BlockSpec(memory_space=pltpu.SMEM)
    hbm = pl.BlockSpec(memory_space=pl.ANY)
    received, all_links = pl.pallas_call(
        functools.partial(exchange_kernel, nblk, bs),
        out_shape=(
            jax.ShapeDtypeStruct((owners, local_scen, bs, bs), BF16),
            jax.ShapeDtypeStruct((owners, 8, 128), jnp.int32),
        ),
        in_specs=[smem, vmem, vmem, hbm, hbm],
        out_specs=(hbm, hbm),
        scratch_shapes=[
            pltpu.VMEM(factor_inv.shape, BF16),
            pltpu.VMEM(border.shape, BF16),
            pltpu.VMEM((8, rows, bs), BF16),
            pltpu.VMEM((8, rows, bs), BF16),
            pltpu.VMEM((2, 2, rows, bs), BF16),
            pltpu.VMEM((2, 8, bs, bs), BF16),
            pltpu.VMEM((2, 8, bs, bs), BF16),
            pltpu.VMEM((8, 128), jnp.int32),
            dma((8,)), dma((8,)), dma((8,)), dma((8,)), dma((4,)), dma((2, 2)),
            dma((2, 4)), dma((2, 8)), dma((8,)), dma((4, 4)), dma((4, 4)), dma((4, 4)),
            dma((7,)), dma((8,)),
        ],
        compiler_params=pltpu.CompilerParams(
            collective_id=0, has_side_effects=True, vmem_limit_bytes=62 * 1024 * 1024
        ),
    )(jnp.transpose(pattern, (1, 0, 2)), row_scale, link_ids.T, factor_inv, border)
    return pl.pallas_call(
        functools.partial(assemble_kernel, group_blocks, owner_blocks, bs),
        out_shape=jax.ShapeDtypeStruct((group_blocks * bs, owner_blocks * bs), F32),
        grid=(group_blocks // 4,),
        in_specs=[smem, hbm, vmem],
        out_specs=pl.BlockSpec((4 * bs, owner_blocks * bs), lambda r: (r, 0)),
        scratch_shapes=[
            pltpu.VMEM(received.shape, BF16),
            pltpu.SMEM((group_blocks,), jnp.int32),
            pltpu.SMEM((owners * local_scen,), jnp.int32),
            pltpu.SMEM((owners * local_scen,), jnp.int32),
            dma,
        ],
        compiler_params=pltpu.CompilerParams(vmem_limit_bytes=62 * 1024 * 1024),
    )(all_links, received, first_diag.reshape(order // bs, bs))


def on_device(factor_inv, *rest):
    sizes = (lax.axis_size("tile"), lax.axis_size("scen"), factor_inv.shape[0])
    form = two_owner_form if sizes == (4, 8, 8) else general_form
    return form(factor_inv, *rest)


def solution(mesh):
    in_specs = (
        P("scen", None, None),
        P("scen", None, None),
        P("scen", None, "tile"),
        P("scen", None),
        P("scen", None),
        P(),
    )
    out_specs = P("tile", "scen")
    return jax.shard_map(
        on_device, mesh=mesh, in_specs=in_specs, out_specs=out_specs, check_vma=False
    )
```
